32 devices in a mesh: groups: 2 (over y), blk: 4 (over z), scen: 2 (over x), month: 2 (over core).
Axes of the slice: x: 2, y: 2, z: 4, core: 2. Of those that a mesh axis runs over, the one named last changes fastest.
Arguments:
- cash_flow: bfloat16 [720, 2048], P('month', ('groups', 'blk')), parts along dimension 1, may hold values from -0.21875 to 0.21875
- fund_units: bfloat16 [720, 2048], P('month', ('groups', 'blk')), parts along dimension 1, may hold values from 0 to 1, as said below
- term_months: int32 [2048], P(('groups', 'blk')), parts along dimension 0, may hold values from 12 to 720, as said below
- cohort: int32 [2048], P(('groups', 'blk')), parts along dimension 0, may hold values from 0 to 63
- guar_type: int32 [2048], P(('groups', 'blk')), parts along dimension 0, may hold values from 0 to 3
- surrender: bfloat16 [2048], P(('groups', 'blk')), parts along dimension 0, may hold values from -3 to 3
- discount: bfloat16 [720, 2048], P(None, ('groups', 'blk', 'scen')), parts along dimension 1, may hold values from 0.02 to 1.2
- fund_index: bfloat16 [720, 2048], P(None, ('groups', 'blk', 'scen')), parts along dimension 1, may hold values from 0.29 to 3
- strike: float32 [4], replicated, may hold values from 0.8 to 2
Outputs:
- cohort_pv: float32 [128, 1024], P('groups', ('blk', 'scen')), parts along dimension 0
- tail_value: float32 [128], P('groups'), parts along dimension 0
The draws below stay inside these ranges and needn't reach their ends.
There are 2 independent parts, one for each index of `groups`. The reference program is written for one: setup_inputs(seed, part) draws one part's arguments, and reference() takes and returns one part's arrays. A program takes and returns all parts, laid end to end along the dimension named above; an argument that names none is the same for every part. Nothing has to cross between parts.
Inputs may be any that keep to these rules, and one draw needn't show every extreme that they name: `term_months`: at least one policy runs all 720 months. `fund_units`: fund units are positive.
All inputs are finite; a program needn't handle non-finite values.
Results may differ from the reference program's by a relative error of at most 0.00049.
Values may be sent and summed in bfloat16 or wider, within the bound.
A program may use at most 128 MiB of HBM per device.

```python
import math
import jax
import jax.numpy as jnp
from jax import lax

M = 720
TYPES = 4
COHORTS = 64
SCEN_DEV = 128
POLICIES = 1024
SCENARIOS = 1024


def draw_term_months(key, part):
    key = jax.random.fold_in(key, 11)
    draw_key, second = jax.random.split(key)
    lowest = max(1, M // 60)
    values = jax.random.randint(draw_key, (POLICIES,), lowest, M + 1, dtype=jnp.int32)
    where_full = jax.random.randint(second, (), 0, POLICIES, dtype=jnp.int32)
    return values.at[where_full].set(M)


def draw_discount(key, part):
    key = jax.random.fold_in(key, 23)
    key_rate, key_jitter = jax.random.split(key)
    position = jnp.arange(SCENARIOS, dtype=jnp.float32) / max(SCENARIOS - 1, 1)
    level = jax.random.uniform(key_rate, (SCENARIOS,), jnp.float32, math.log(0.7), math.log(1.4))
    rates_short = 0.01 * (1.0 + 3.0 * position) * jnp.exp(level)
    years = (jnp.arange(M, dtype=jnp.float32) + 1.0) / 12.0
    jitter = jax.random.uniform(key_jitter, (M, SCENARIOS), jnp.float32, 0.8, 1.2)
    return (jnp.exp(-years[:, None] * rates_short[None, :]) * jitter).astype(jnp.bfloat16)


def draw_fund_index(key, part):
    key = jax.random.fold_in(key, 37)
    key_block, key_scen, key_jitter, key_crash = jax.random.split(key, 4)
    blocks = SCENARIOS // SCEN_DEV
    block_level = jax.random.uniform(key_block, (blocks, 1), jnp.float32, -0.25, 0.25)
    scen_level = jax.random.uniform(key_scen, (blocks, SCEN_DEV), jnp.float32, -0.12, 0.12)
    level = (block_level + scen_level).reshape(SCENARIOS)
    jitter = jax.random.uniform(key_jitter, (M, SCENARIOS), jnp.float32, -0.28, 0.28)
    base = 1.3
    values = base * jnp.exp(level[None, :] + jitter)
    crash = jax.random.randint(key_crash, (SCENARIOS,), 0, 200, dtype=jnp.int32) == 0
    values = jnp.where(crash[None, :], 0.3125, values)
    return jnp.clip(values, 0.3125, 3.0).astype(jnp.bfloat16)


def draw_fund_units(key, part):
    key = jax.random.fold_in(key, 41)
    key_policy, key_month = jax.random.split(key)
    policy_scale = jnp.exp(jax.random.uniform(key_policy, (POLICIES,), jnp.float32, math.log(0.3), math.log(3.0)))
    month_factor = jax.random.uniform(key_month, (M, POLICIES), jnp.float32, 0.5, 1.5)
    return (policy_scale[None, :] * month_factor / M).astype(jnp.bfloat16)


def touch_ends(entries, rng, least, top_value):
    longest = entries.shape.index(max(entries.shape))
    spots = []
    for shift in (0, 1):
        where = [jax.random.randint(jax.random.fold_in(rng, axis), (), 0, length) for axis, length in enumerate(entries.shape)]
        where[longest] = (where[longest] + shift) % entries.shape[longest]
        spots.append(tuple(where))
    return entries.at[spots[0]].set(least).at[spots[1]].set(top_value)


def levels(stream_key, extent, cuts, low, top_value):
    factor_of, own = 1.0, jax.random.fold_in(stream_key, 6)
    for dim, blocks in cuts:
        steps = jnp.exp(jax.random.uniform(jax.random.fold_in(own, dim), (blocks,), jnp.float32, low / len(cuts), top_value / len(cuts)))
        factor_of = factor_of * jnp.repeat(steps, extent[dim] // blocks).reshape([-1 if axis == dim else 1 for axis in range(len(extent))])
    return factor_of


def centred(key, extent, width, bound, shards=(), kind=jnp.bfloat16):
    drawn = jax.random.normal(key, extent, jnp.float32) * width
    if len(shards) > 0:
        drawn = levels(key, extent, shards, -0.22, 0.18) * drawn
    return jnp.clip(drawn, min=-bound, max=bound).astype(kind)


def setup_inputs(seed: int = 0, part: int = 0) -> dict:
    arg_keys = jax.random.split(jax.random.key(seed), 10)
    part_keys = jax.random.split(jax.random.fold_in(arg_keys[9], part), 10)
    return {
        "cash_flow": centred(part_keys[0], (M, POLICIES), M ** -0.5, 0.21875, ((0, 2), (1, 4))),
        "fund_units": draw_fund_units(jax.random.fold_in(jax.random.fold_in(arg_keys[9], part), 71), part),
        "term_months": draw_term_months(jax.random.fold_in(jax.random.fold_in(arg_keys[9], part), 71), part),
        "cohort": touch_ends(jax.random.randint(part_keys[3], (POLICIES,), 0, COHORTS), jax.random.fold_in(part_keys[3], 1), 0, COHORTS - 1).astype(jnp.int32),
        "guar_type": touch_ends(jax.random.randint(part_keys[4], (POLICIES,), 0, TYPES), jax.random.fold_in(part_keys[4], 1), 0, TYPES - 1).astype(jnp.int32),
        "surrender": centred(part_keys[5], (POLICIES,), 0.5, 3.0, ((0, 4),)),
        "discount": draw_discount(jax.random.fold_in(jax.random.fold_in(arg_keys[9], part), 71), part),
        "fund_index": draw_fund_index(jax.random.fold_in(jax.random.fold_in(arg_keys[9], part), 71), part),
        "strike": jnp.clip(jax.random.uniform(arg_keys[8], (TYPES,), jnp.float32, 0.8, 2.0), 0.8, 2.0),
    }


def reference(cash_flow, fund_units, term_months, cohort, guar_type, surrender, discount, fund_index, strike):
    month_index = jnp.arange(M, dtype=jnp.int32)[:, None]
    in_force = month_index < term_months[None, :]
    cash_flows = jnp.where(in_force, cash_flow, jnp.zeros_like(cash_flow))
    fund_held = jnp.where(in_force, fund_units, jnp.zeros_like(fund_units))
    type_hot = (guar_type[:, None] == jnp.arange(TYPES, dtype=jnp.int32)[None, :]).astype(jnp.float32)
    cohort_hot = (cohort[:, None] == jnp.arange(COHORTS, dtype=jnp.int32)[None, :]).astype(jnp.float32)
    floor_value = surrender.astype(jnp.float32)
    scaling = 1.0 / math.sqrt(POLICIES / COHORTS)
    scen_block = math.gcd(512, SCENARIOS)
    block_count = SCENARIOS // scen_block
    disc_blocks = discount.reshape(M, block_count, scen_block).transpose(1, 0, 2)
    index_blocks = fund_index.reshape(M, block_count, scen_block).transpose(1, 0, 2)

    def cohort_block(pair_arrays):
        discounts, index_values = pair_arrays
        payoffs = jnp.maximum(strike.astype(jnp.float32)[:, None, None] - index_values.astype(jnp.float32)[None], 0.0).astype(jnp.bfloat16)
        payoffs = payoffs.transpose(1, 0, 2).reshape(M, TYPES * scen_block)
        net_value = lax.dot_general(cash_flows, discounts, (((0,), (0,)), ((), ())), preferred_element_type=jnp.float32)
        guar_all = lax.dot_general(fund_held, payoffs, (((0,), (0,)), ((), ())), preferred_element_type=jnp.float32)
        guar_all = guar_all.reshape(POLICIES, TYPES, scen_block)
        guarantee = lax.optimization_barrier(jnp.sum(type_hot[:, :, None] * guar_all, axis=1))
        policy_value = jnp.maximum(net_value + guarantee, floor_value[:, None])
        return jnp.dot(cohort_hot.T, policy_value, precision=lax.Precision.HIGHEST, preferred_element_type=jnp.float32)
    results = lax.map(cohort_block, (disc_blocks, index_blocks))
    cohort_pv = results.transpose(1, 0, 2).reshape(COHORTS, SCENARIOS) * scaling
    totals = lax.optimization_barrier(jnp.sum(cohort_pv, axis=1))
    squares = lax.optimization_barrier(jnp.sum(cohort_pv * cohort_pv, axis=1))
    centre = totals / SCENARIOS
    spread = squares / SCENARIOS - centre * centre
    temper = 0.5 * jnp.sqrt(spread + 1e-05)
    weights = jax.nn.sigmoid((cohort_pv - centre[:, None]) / temper[:, None])
    tail_value = lax.optimization_barrier(jnp.sum(weights * cohort_pv, axis=1)) / lax.optimization_barrier(jnp.sum(weights, axis=1))
    return (cohort_pv, tail_value)
```

```python
import functools
import math

import jax
import jax.numpy as jnp
from jax import lax
from jax.experimental import pallas as pl
from jax.experimental.pallas import tpu as pltpu
from jax.sharding import PartitionSpec as P

COHORTS = 64
MESH = pl.DeviceIdType.MESH
BF16 = jnp.bfloat16
F32 = jnp.float32


def remote(src, dst, send_sem, recv_sem, **where):
    return pltpu.make_async_remote_copy(
        src_ref=src,
        dst_ref=dst,
        send_sem=send_sem,
        recv_sem=recv_sem,
        device_id=where,
        device_id_type=MESH,
    )


def kernel(
    n,
    nx,
    scaling,
    cash_ref,
    fund_ref,
    term_ref,
    cohort_ref,
    type_ref,
    floor_ref,
    disc_ref,
    index_ref,
    strike_ref,
    pv_ref,
    tail_ref,
    pol,
    scen,
    lhs,
    hot,
    kind,
    floor,
    part,
    red,
    pv,
    stat,
    tails,
    pol_local,
    pol_send,
    pol_recv,
    own_local,
    scen_send,
    scen_recv,
    red_send,
    red_recv,
    pv_send,
    pv_recv,
    stat_send,
    stat_recv,
    tail_send,
    tail_recv,
):
    z = lax.axis_index("blk")
    x = lax.axis_index("scen")
    core = lax.axis_index("month")
    other = 1 - core
    h = n // 2
    low = core * h
    half, pols = cash_ref.shape
    months, lanes = disc_ref.shape
    types = strike_ref.shape[0]
    depth = lhs.shape[2]
    rows = COHORTS // 2
    scen_total = n * nx * lanes
    peers = n * nx
    me = z * nx + x
    gid = me * 2 + core

    barrier = pltpu.get_barrier_semaphore()

    def greet(i, carry):
        to = lax.rem(gid + i, 2 * peers)
        pl.semaphore_signal(
            barrier,
            inc=1,
            device_id={"blk": to // (2 * nx), "scen": lax.rem(to // 2, nx), "month": lax.rem(to, 2)},
            device_id_type=MESH,
        )
        return carry

    lax.fori_loop(1, 2 * peers, greet, 0)
    own_pol = [
        pltpu.make_async_copy(ref, pol.at[core, a], pol_local.at[a])
        for a, ref in enumerate((cash_ref, fund_ref))
    ]
    for copy in own_pol:
        copy.start()
    mine = (z >= low) & (z < low + h)

    def own_scen(a):
        ref = (disc_ref, index_ref)[a]
        return pltpu.make_async_copy(ref, scen.at[z - low, a], own_local.at[a])

    @pl.when(mine)
    def _():
        for a in range(2):
            own_scen(a).start()

    pl.semaphore_wait(barrier, 2 * peers - 1)

    def hop(src, j, a, right):
        return remote(
            src,
            scen.at[j, a],
            scen_send.at[j, a, right],
            scen_recv.at[j, a],
            blk=z + (1 if right else -1),
        )

    for a, ref in enumerate((disc_ref, index_ref)):
        @pl.when(mine & (z < n - 1))
        def _():
            hop(ref, z - low, a, 1).start()

        @pl.when(mine & (z > 0))
        def _():
            hop(ref, z - low, a, 0).start()

    give_pol = [
        remote(ref, pol.at[core, a], pol_send.at[a], pol_recv.at[a], month=other)
        for a, ref in enumerate((cash_ref, fund_ref))
    ]
    for copy in give_pol:
        copy.start()

    term = term_ref[...].reshape(1, pols)
    month = lax.broadcasted_iota(jnp.int32, (depth, pols), 0)
    in_force = month < term
    cohort_row = cohort_ref[...].reshape(1, pols)
    hot[...] = jnp.where(
        lax.broadcasted_iota(jnp.int32, (COHORTS, pols), 0) == cohort_row, 1.0, 0.0
    ).astype(BF16)
    kind[...] = jnp.broadcast_to(type_ref[...].reshape(1, pols).astype(F32), (lanes, pols)).T
    floor[...] = jnp.broadcast_to(floor_ref[...].astype(F32).reshape(1, pols), (lanes, pols)).T
    for a in range(2):
        own_pol[a].wait()
        remote(
            pol.at[other, a], pol.at[other, a], pol_send.at[a], pol_recv.at[a], month=other
        ).wait_recv()
        held = jnp.concatenate(
            [
                pol[0, a].astype(F32),
                pol[1, a].astype(F32),
                jnp.zeros((depth - months, pols), F32),
            ],
            axis=0,
        )
        lhs[a] = jnp.where(in_force, held, 0.0).T.astype(BF16)

    def cohort_terms(j):
        pad = jnp.zeros((depth - months, lanes), BF16)
        disc = jnp.concatenate([scen[j, 0], pad], axis=0)
        net = jnp.dot(lhs[0], disc, preferred_element_type=F32)
        index = scen[j, 1].astype(F32)
        pays = jnp.concatenate(
            [
                jnp.concatenate(
                    [jnp.maximum(strike_ref[t] - index, 0.0).astype(BF16), pad], axis=0
                )
                for t in range(types)
            ],
            axis=1,
        )
        every = jnp.dot(lhs[1], pays, preferred_element_type=F32)
        which = kind[...]
        guarantee = every[:, :lanes]
        for t in range(1, types):
            guarantee = jnp.where(which == t, every[:, t * lanes : (t + 1) * lanes], guarantee)
        value = jnp.maximum(net + guarantee, floor[...])
        high = value.astype(BF16)
        rest = value - high.astype(F32)
        middle = rest.astype(BF16)
        least = (rest - middle.astype(F32)).astype(BF16)
        sums = jnp.dot(
            hot[...], jnp.concatenate([high, middle, least], axis=1), preferred_element_type=F32
        )
        return sums[:, :lanes] + sums[:, lanes : 2 * lanes] + sums[:, 2 * lanes :]

    def give_red(j, to):
        return remote(
            part.at[j, to],
            red.at[z],
            red_send.at[j, to],
            red_recv.at[z],
            blk=low + j,
            month=jnp.int32(to),
        )

    def step(t, carry):
        d = (t + 1) // 2
        b = jnp.where(lax.rem(t, 2) == 1, z - d, z + d)
        j = b - low

        @pl.when((j >= 0) & (j < h))
        def _():
            @pl.when(b == z)
            def _():
                for a in range(2):
                    own_scen(a).wait()

            for a in range(2):
                @pl.when(b < z)
                def _():
                    hop(scen.at[j, a], j, a, 1).wait_recv()

                @pl.when(b > z)
                def _():
                    hop(scen.at[j, a], j, a, 0).wait_recv()

                @pl.when((b < z) & (z < n - 1))
                def _():
                    hop(scen.at[j, a], j, a, 1).start()

                @pl.when((b > z) & (z > 0))
                def _():
                    hop(scen.at[j, a], j, a, 0).start()

            sums = cohort_terms(j)
            part[j, 0] = sums[:rows]
            part[j, 1] = sums[rows:]
            for to in range(2):
                @pl.when((b == z) & (core == to))
                def _():
                    red[z] = part[j, to]

                @pl.when((b != z) | (core != to))
                def _():
                    give_red(j, to).start()

        return carry

    lax.fori_loop(0, 2 * n - 1, step, 0)

    owner = z // h

    def take_red(i, carry):
        @pl.when((i != z) | (core != owner))
        def _():
            remote(
                red.at[i], red.at[i], red_send.at[0, 0], red_recv.at[i], month=other
            ).wait_recv()

        return carry

    lax.fori_loop(0, n, take_red, 0)
    own = red[0]
    for i in range(1, n):
        own = own + red[i]
    own = own * scaling
    pv[core] = own
    give_pv = remote(pv.at[core], pv.at[core], pv_send.at[0], pv_recv.at[0], month=other)
    give_pv.start()

    line = lax.broadcasted_iota(jnp.int32, (lanes, lanes), 0)
    wide = jnp.concatenate([own, own, jnp.zeros((lanes - 2 * rows, lanes), F32)], axis=0)
    turned = jnp.where(line // rows == core, wide, 0.0).T
    stat[me] = jnp.concatenate(
        [
            jnp.sum(turned, axis=0, keepdims=True),
            jnp.sum(turned * turned, axis=0, keepdims=True),
        ],
        axis=0,
    )

    def give_stat(i):
        to = lax.rem(me + i, peers)
        return remote(
            stat.at[me],
            stat.at[me],
            stat_send.at[i],
            stat_recv.at[me],
            blk=to // nx,
            scen=lax.rem(to, nx),
        )

    def take_stat(i, carry):
        to = lax.rem(me + i, peers)
        remote(
            stat.at[to],
            stat.at[to],
            stat_send.at[i],
            stat_recv.at[to],
            blk=to // nx,
            scen=lax.rem(to, nx),
        ).wait_recv()
        return carry

    def each(first, last, action):
        def go(i, carry):
            action(i)
            return carry

        lax.fori_loop(first, last, go, 0)

    each(1, peers, lambda i: give_stat(i).start())
    lax.fori_loop(1, peers, take_stat, 0)
    stats = jnp.sum(stat[...], axis=0)
    centre = stats[0:1] / scen_total
    spread = stats[1:2] / scen_total - centre * centre
    temper = 0.5 * jnp.sqrt(spread + 1e-05)
    weights = jax.nn.sigmoid((turned - centre) / temper)
    column = lax.broadcasted_iota(jnp.int32, (1, lanes), 1)
    lower = jnp.where(column // rows == core, jnp.sum(weights, axis=0, keepdims=True), 0.0)
    upper = jnp.sum(weights * turned, axis=0, keepdims=True)
    tails[gid] = jnp.concatenate([upper, lower], axis=0)

    def give_tail(i):
        to = lax.rem(gid + i, 2 * peers)
        return remote(
            tails.at[gid],
            tails.at[gid],
            tail_send.at[i],
            tail_recv.at[gid],
            blk=to // (2 * nx),
            scen=lax.rem(to // 2, nx),
            month=lax.rem(to, 2),
        )

    def take_tail(i):
        to = lax.rem(gid + i, 2 * peers)
        return remote(
            tails.at[to],
            tails.at[to],
            tail_send.at[i],
            tail_recv.at[to],
            blk=to // (2 * nx),
            scen=lax.rem(to // 2, nx),
            month=lax.rem(to, 2),
        )

    each(1, 2 * peers, lambda i: give_tail(i).start())

    remote(
        pv.at[other], pv.at[other], pv_send.at[0], pv_recv.at[0], month=other
    ).wait_recv()
    pv_ref[:rows] = pv[0]
    pv_ref[rows:] = pv[1]
    give_pv.wait_send()
    for copy in give_pol:
        copy.wait_send()

    def finish(j, carry):
        b = low + j
        for a in range(2):
            @pl.when((b <= z) & (z < n - 1))
            def _():
                hop(scen.at[j, a], j, a, 1).wait_send()

            @pl.when((b >= z) & (z > 0))
            def _():
                hop(scen.at[j, a], j, a, 0).wait_send()

        for to in range(2):
            @pl.when((b != z) | (core != to))
            def _():
                give_red(j, to).wait_send()

        return carry

    lax.fori_loop(0, h, finish, 0)
    each(1, peers, lambda i: give_stat(i).wait_send())

    each(1, 2 * peers, lambda i: take_tail(i).wait_recv())
    sums = jnp.sum(tails[...], axis=0)
    tail_ref[...] = (sums[0:1] / sums[1:2])[:, :COHORTS]
    each(1, 2 * peers, lambda i: give_tail(i).wait_send())


def per_device(
    cash_flow, fund_units, term_months, cohort, guar_type, surrender, discount, fund_index, strike
):
    n, nx = lax.axis_size("blk"), lax.axis_size("scen")
    half, pols = cash_flow.shape
    months, lanes = discount.shape
    h = n // 2
    rows = COHORTS // 2
    peers = n * nx
    depth = -(-months // 256) * 256
    scaling = 1.0 / math.sqrt(pols * n / COHORTS)
    vmem = pl.BlockSpec(memory_space=pltpu.VMEM)
    hbm = pl.BlockSpec(memory_space=pl.ANY)
    smem = pl.BlockSpec(memory_space=pltpu.SMEM)
    dma = pltpu.SemaphoreType.DMA
    cohort_pv, tail = pl.pallas_call(
        functools.partial(kernel, n, nx, scaling),
        out_shape=(
            jax.ShapeDtypeStruct((COHORTS, lanes), F32),
            jax.ShapeDtypeStruct((1, COHORTS), F32),
        ),
        in_specs=[hbm, hbm, vmem, vmem, vmem, vmem, hbm, hbm, smem],
        out_specs=(vmem, vmem),
        scratch_shapes=[
            pltpu.VMEM((2, 2, half, pols), BF16),
            pltpu.VMEM((h, 2, months, lanes), BF16),
            pltpu.VMEM((2, pols, depth), BF16),
            pltpu.VMEM((COHORTS, pols), BF16),
            pltpu.VMEM((pols, lanes), F32),
            pltpu.VMEM((pols, lanes), F32),
            pltpu.VMEM((h, 2, rows, lanes), F32),
            pltpu.VMEM((n, rows, lanes), F32),
            pltpu.VMEM((2, rows, lanes), F32),
            pltpu.VMEM((peers, 2, lanes), F32),
            pltpu.VMEM((2 * peers, 2, lanes), F32),
            dma((2,)),
            dma((2,)),
            dma((2,)),
            dma((2,)),
            dma((h, 2, 2)),
            dma((h, 2)),
            dma((h, 2)),
            dma((n,)),
            dma((1,)),
            dma((1,)),
            dma((peers,)),
            dma((peers,)),
            dma((2 * peers,)),
            dma((2 * peers,)),
        ],
        compiler_params=pltpu.CompilerParams(
            collective_id=0, has_side_effects=True, vmem_limit_bytes=32 * 1024 * 1024
        ),
        cost_estimate=pl.CostEstimate(
            flops=10 * pols * h * lanes * months, bytes_accessed=1 << 20, transcendentals=0
        ),
    )(
        cash_flow,
        fund_units,
        term_months.reshape(1, pols),
        cohort.reshape(1, pols),
        guar_type.reshape(1, pols),
        surrender.reshape(1, pols),
        discount,
        fund_index,
        strike,
    )
    return cohort_pv, tail.reshape(COHORTS)


def solution(mesh):
    return jax.shard_map(
        per_device,
        mesh=mesh,
        in_specs=(
            P("month", ("groups", "blk")),
            P("month", ("groups", "blk")),
            P(("groups", "blk")),
            P(("groups", "blk")),
            P(("groups", "blk")),
            P(("groups", "blk")),
            P(None, ("groups", "blk", "scen")),
            P(None, ("groups", "blk", "scen")),
            P(),
        ),
        out_specs=(P("groups", ("blk", "scen")), P("groups")),
        check_vma=False,
    )
```

```python
import functools
import math

import jax
import jax.numpy as jnp
from jax import lax
from jax.experimental import pallas as pl
from jax.experimental.pallas import tpu as pltpu
from jax.sharding import PartitionSpec as P

COHORTS = 64
MESH = pl.DeviceIdType.MESH
BF16 = jnp.bfloat16
F32 = jnp.float32


def remote(src, dst, send_sem, recv_sem, **where):
    return pltpu.make_async_remote_copy(
        src_ref=src,
        dst_ref=dst,
        send_sem=send_sem,
        recv_sem=recv_sem,
        device_id=where,
        device_id_type=MESH,
    )


def kernel(
    n,
    nx,
    scaling,
    cash_ref,
    fund_ref,
    term_hbm,
    cohort_hbm,
    type_hbm,
    floor_hbm,
    disc_ref,
    index_ref,
    strike_hbm,
    pv_ref,
    tail_ref,
    pol,
    scen,
    lhs,
    hot,
    kind,
    floor,
    part,
    red,
    pv,
    stat,
    tails,
    pol_local,
    pol_send,
    pol_recv,
    own_local,
    scen_send,
    scen_recv,
    red_send,
    red_recv,
    pv_send,
    pv_recv,
    stat_send,
    stat_recv,
    tail_send,
    tail_recv,
    final,
    term_ref,
    cohort_ref,
    type_ref,
    floor_ref,
    strike_ref,
    small_local,
):
    z = lax.axis_index("blk")
    x = lax.axis_index("scen")
    core = lax.axis_index("month")
    other = 1 - core
    h = n // 2
    low = core * h
    half, pols = cash_ref.shape
    months, lanes = disc_ref.shape
    types = strike_hbm.shape[0]
    depth = lhs.shape[2]
    first = -(-months // 32) * 16
    pieces = ((0, first), (first, months - first))
    chunks = [(a, k) for k in range(2) for a in range(2)]
    scen_total = n * nx * lanes
    peers = n * nx
    me = z * nx + x

    barrier = pltpu.get_barrier_semaphore()

    def greet(**where):
        pl.semaphore_signal(barrier, inc=1, device_id=where, device_id_type=MESH)

    greet(month=other)

    @pl.when(core == 0)
    def _():
        @pl.when(z > 0)
        def _():
            greet(blk=z - 1)

        @pl.when(z < n - 1)
        def _():
            greet(blk=z + 1)

    @pl.when(core == 1)
    def _():
        def peer(i, carry):
            to = lax.rem(me + i, peers)
            greet(blk=to // nx, scen=lax.rem(to, nx))
            return carry

        lax.fori_loop(1, peers, peer, 0)

        def line_peer(i, carry):
            greet(blk=lax.rem(z + i, n), month=jnp.int32(0))
            return carry

        lax.fori_loop(1, n, line_peer, 0)

    small = [
        pltpu.make_async_copy(src, dst, small_local.at[k])
        for k, (src, dst) in enumerate(
            (
                (term_hbm, term_ref),
                (cohort_hbm, cohort_ref),
                (type_hbm, type_ref),
                (floor_hbm, floor_ref),
                (strike_hbm, strike_ref),
            )
        )
    ]
    for copy in small:
        copy.start()
    own_pol = [
        pltpu.make_async_copy(ref, pol.at[core, a], pol_local.at[a])
        for a, ref in enumerate((cash_ref, fund_ref))
    ]
    for copy in own_pol:
        copy.start()
    mine = (z >= low) & (z < low + h)

    def own_scen(a):
        ref = (disc_ref, index_ref)[a]
        return pltpu.make_async_copy(ref, scen.at[z - low, a], own_local.at[a])

    @pl.when(mine)
    def _():
        for a in range(2):
            own_scen(a).start()

    around = jnp.where(z > 0, 1, 0) + jnp.where(z < n - 1, 1, 0)
    pl.semaphore_wait(barrier, jnp.where(core == 1, peers, n + around))

    def piece(ref, k):
        return ref.at[pl.ds(pieces[k][0], pieces[k][1])]

    def hop(src, j, a, k, right):
        return remote(
            piece(src, k),
            piece(scen.at[j, a], k),
            scen_send.at[j, a, k, right],
            scen_recv.at[j, a, k],
            blk=z + (1 if right else -1),
        )

    for a, k in chunks:
        ref = (disc_ref, index_ref)[a]

        @pl.when(mine & (z < n - 1))
        def _():
            hop(ref, z - low, a, k, 1).start()

        @pl.when(mine & (z > 0))
        def _():
            hop(ref, z - low, a, k, 0).start()

    give_pol = [
        remote(ref, pol.at[core, a], pol_send.at[a], pol_recv.at[a], month=other)
        for a, ref in enumerate((cash_ref, fund_ref))
    ]
    for copy in give_pol:
        copy.start()

    for copy in small:
        copy.wait()
    term = term_ref[...].reshape(1, pols)
    month = lax.broadcasted_iota(jnp.int32, (depth, pols), 0)
    in_force = month < term
    cohort_row = cohort_ref[...].reshape(1, pols)
    hot[...] = jnp.where(
        lax.broadcasted_iota(jnp.int32, (COHORTS, pols), 0) == cohort_row, 1.0, 0.0
    ).astype(BF16)
    kind[...] = jnp.broadcast_to(type_ref[...].reshape(1, pols).astype(F32), (lanes, pols)).T
    floor[...] = jnp.broadcast_to(floor_ref[...].astype(F32).reshape(1, pols), (lanes, pols)).T
    for a in range(2):
        own_pol[a].wait()
        remote(
            pol.at[other, a], pol.at[other, a], pol_send.at[a], pol_recv.at[a], month=other
        ).wait_recv()
        held = jnp.concatenate(
            [
                pol[0, a].astype(F32),
                pol[1, a].astype(F32),
                jnp.zeros((depth - months, pols), F32),
            ],
            axis=0,
        )
        lhs[a] = jnp.where(in_force, held, 0.0).T.astype(BF16)

    def cohort_terms(j):
        pad = jnp.zeros((depth - months, lanes), BF16)
        disc = jnp.concatenate([scen[j, 0], pad], axis=0)
        net = jnp.dot(lhs[0], disc, preferred_element_type=F32)
        index = scen[j, 1].astype(F32)
        pays = jnp.concatenate(
            [
                jnp.concatenate(
                    [jnp.maximum(strike_ref[t] - index, 0.0).astype(BF16), pad], axis=0
                )
                for t in range(types)
            ],
            axis=1,
        )
        every = jnp.dot(lhs[1], pays, preferred_element_type=F32)
        which = kind[...]
        guarantee = every[:, :lanes]
        for t in range(1, types):
            guarantee = jnp.where(which == t, every[:, t * lanes : (t + 1) * lanes], guarantee)
        value = jnp.maximum(net + guarantee, floor[...])
        high = value.astype(BF16)
        rest = value - high.astype(F32)
        middle = rest.astype(BF16)
        least = (rest - middle.astype(F32)).astype(BF16)
        sums = jnp.dot(
            hot[...], jnp.concatenate([high, middle, least], axis=1), preferred_element_type=F32
        )
        return sums[:, :lanes] + sums[:, lanes : 2 * lanes] + sums[:, 2 * lanes :]

    def give_red(j):
        return remote(
            part.at[j], red.at[z], red_send.at[j], red_recv.at[z], blk=low + j, month=jnp.int32(1)
        )

    def step(t, carry):
        d = (t + 1) // 2
        b = jnp.where(lax.rem(t, 2) == 1, z - d, z + d)
        j = b - low

        @pl.when((j >= 0) & (j < h))
        def _():
            @pl.when(b == z)
            def _():
                for a in range(2):
                    own_scen(a).wait()

            for a, k in chunks:
                @pl.when(b < z)
                def _():
                    hop(scen.at[j, a], j, a, k, 1).wait_recv()

                @pl.when(b > z)
                def _():
                    hop(scen.at[j, a], j, a, k, 0).wait_recv()

                @pl.when((b < z) & (z < n - 1))
                def _():
                    hop(scen.at[j, a], j, a, k, 1).start()

                @pl.when((b > z) & (z > 0))
                def _():
                    hop(scen.at[j, a], j, a, k, 0).start()

            sums = cohort_terms(j)
            part[j] = sums

            @pl.when((b == z) & (core == 1))
            def _():
                red[z] = sums

            @pl.when((b != z) | (core != 1))
            def _():
                give_red(j).start()

        return carry

    lax.fori_loop(0, 2 * n - 1, step, 0)

    give_pv = remote(pv, pv, pv_send.at[0], pv_recv.at[0], month=other)
    give_final = remote(final, final, pv_send.at[1], pv_recv.at[1], month=other)

    def each(first, last, action):
        def go(i, carry):
            action(i)
            return carry

        lax.fori_loop(first, last, go, 0)

    def share(ref, send_sem, recv_sem, i, slot):
        to = lax.rem(me + i, peers)
        where = slot(to)
        return remote(
            ref.at[where],
            ref.at[where],
            send_sem.at[i],
            recv_sem.at[where],
            blk=to // nx,
            scen=lax.rem(to, nx),
        )

    def give(ref, send_sem, recv_sem, i):
        return share(ref, send_sem, recv_sem, i, lambda to: me)

    def take(ref, send_sem, recv_sem, i):
        return share(ref, send_sem, recv_sem, i, lambda to: to)

    @pl.when(core == 1)
    def _():
        owner = z // h

        def take_red(i):
            @pl.when((i != z) | (owner != 1))
            def _():
                remote(red.at[i], red.at[i], red_send.at[0], red_recv.at[i], month=other).wait_recv()

        each(0, n, take_red)
        own = red[0]
        for i in range(1, n):
            own = own + red[i]
        own = own * scaling
        turned = jnp.concatenate([own, jnp.zeros((lanes - COHORTS, lanes), F32)], axis=0).T
        stat[me] = jnp.concatenate(
            [
                jnp.sum(turned, axis=0, keepdims=True),
                jnp.sum(turned * turned, axis=0, keepdims=True),
            ],
            axis=0,
        )
        each(1, peers, lambda i: give(stat, stat_send, stat_recv, i).start())
        pv[...] = own
        give_pv.start()
        pv_ref[...] = own
        each(1, peers, lambda i: take(stat, stat_send, stat_recv, i).wait_recv())
        stats = jnp.sum(stat[...], axis=0)
        centre = stats[0:1] / scen_total
        spread = stats[1:2] / scen_total - centre * centre
        temper = 0.5 * jnp.sqrt(spread + 1e-05)
        weights = jax.nn.sigmoid((turned - centre) / temper)
        tails[me] = jnp.concatenate(
            [
                jnp.sum(weights * turned, axis=0, keepdims=True),
                jnp.sum(weights, axis=0, keepdims=True),
            ],
            axis=0,
        )
        each(1, peers, lambda i: give(tails, tail_send, tail_recv, i).start())
        each(1, peers, lambda i: give(stat, stat_send, stat_recv, i).wait_send())
        give_pv.wait_send()
        each(1, peers, lambda i: take(tails, tail_send, tail_recv, i).wait_recv())
        ends = jnp.sum(tails[...], axis=0)
        final[...] = ends[0:1] / ends[1:2]
        give_final.start()

    for copy in give_pol:
        copy.wait_send()

    def finish(j, carry):
        b = low + j
        for a, k in chunks:
            @pl.when((b <= z) & (z < n - 1))
            def _():
                hop(scen.at[j, a], j, a, k, 1).wait_send()

            @pl.when((b >= z) & (z > 0))
            def _():
                hop(scen.at[j, a], j, a, k, 0).wait_send()

        @pl.when((b != z) | (core != 1))
        def _():
            give_red(j).wait_send()

        return carry

    lax.fori_loop(0, h, finish, 0)

    @pl.when(core == 1)
    def _():
        each(1, peers, lambda i: give(tails, tail_send, tail_recv, i).wait_send())
        give_final.wait_send()

    @pl.when(core == 0)
    def _():
        give_pv.wait_recv()
        pv_ref[...] = pv[...]
        give_final.wait_recv()

    tail_ref[...] = final[:, :COHORTS]


def per_device(
    cash_flow, fund_units, term_months, cohort, guar_type, surrender, discount, fund_index, strike
):
    n, nx = lax.axis_size("blk"), lax.axis_size("scen")
    half, pols = cash_flow.shape
    months, lanes = discount.shape
    h = n // 2
    peers = n * nx
    depth = -(-months // 256) * 256
    scaling = 1.0 / math.sqrt(pols * n / COHORTS)
    vmem = pl.BlockSpec(memory_space=pltpu.VMEM)
    hbm = pl.BlockSpec(memory_space=pltpu.HBM)
    dma = pltpu.SemaphoreType.DMA
    cohort_pv, tail = pl.pallas_call(
        functools.partial(kernel, n, nx, scaling),
        out_shape=(
            jax.ShapeDtypeStruct((COHORTS, lanes), F32),
            jax.ShapeDtypeStruct((1, COHORTS), F32),
        ),
        in_specs=[hbm] * 9,
        out_specs=(vmem, vmem),
        scratch_shapes=[
            pltpu.VMEM((2, 2, half, pols), BF16),
            pltpu.VMEM((h, 2, months, lanes), BF16),
            pltpu.VMEM((2, pols, depth), BF16),
            pltpu.VMEM((COHORTS, pols), BF16),
            pltpu.VMEM((pols, lanes), F32),
            pltpu.VMEM((pols, lanes), F32),
            pltpu.VMEM((h, COHORTS, lanes), F32),
            pltpu.VMEM((n, COHORTS, lanes), F32),
            pltpu.VMEM((COHORTS, lanes), F32),
            pltpu.VMEM((peers, 2, lanes), F32),
            pltpu.VMEM((peers, 2, lanes), F32),
            dma((2,)),
            dma((2,)),
            dma((2,)),
            dma((2,)),
            dma((h, 2, 2, 2)),
            dma((h, 2, 2)),
            dma((h,)),
            dma((n,)),
            dma((2,)),
            dma((2,)),
            dma((peers,)),
            dma((peers,)),
            dma((peers,)),
            dma((peers,)),
            pltpu.VMEM((1, lanes), F32),
            pltpu.VMEM((pols,), jnp.int32),
            pltpu.VMEM((pols,), jnp.int32),
            pltpu.VMEM((pols,), jnp.int32),
            pltpu.VMEM((pols,), BF16),
            pltpu.SMEM((strike.shape[0],), F32),
            dma((5,)),
        ],
        compiler_params=pltpu.CompilerParams(
            collective_id=0, has_side_effects=True, vmem_limit_bytes=56 * 1024 * 1024
        ),
        cost_estimate=pl.CostEstimate(
            flops=10 * pols * h * lanes * months, bytes_accessed=1 << 20, transcendentals=0
        ),
    )(
        cash_flow,
        fund_units,
        term_months,
        cohort,
        guar_type,
        surrender,
        discount,
        fund_index,
        strike,
    )
    return cohort_pv, tail.reshape(COHORTS)


def solution(mesh):
    return jax.shard_map(
        per_device,
        mesh=mesh,
        in_specs=(
            P("month", ("groups", "blk")),
            P("month", ("groups", "blk")),
            P(("groups", "blk")),
            P(("groups", "blk")),
            P(("groups", "blk")),
            P(("groups", "blk")),
            P(None, ("groups", "blk", "scen")),
            P(None, ("groups", "blk", "scen")),
            P(),
        ),
        out_specs=(P("groups", ("blk", "scen")), P("groups")),
        check_vma=False,
    )
```

```python
import functools
import math

import jax
import jax.numpy as jnp
from jax import lax
from jax.experimental import pallas as pl
from jax.experimental.pallas import tpu as pltpu
from jax.sharding import PartitionSpec as P

COHORTS = 64
MESH = pl.DeviceIdType.MESH
BF16 = jnp.bfloat16
F32 = jnp.float32


def remote(src, dst, send_sem, recv_sem, **where):
    return pltpu.make_async_remote_copy(
        src_ref=src,
        dst_ref=dst,
        send_sem=send_sem,
        recv_sem=recv_sem,
        device_id=where,
        device_id_type=MESH,
    )


def kernel(
    n,
    nx,
    scaling,
    cash_ref,
    fund_ref,
    term_hbm,
    cohort_hbm,
    type_hbm,
    floor_hbm,
    disc_ref,
    index_ref,
    strike_hbm,
    pv_ref,
    tail_ref,
    pol,
    scen,
    lhs,
    hot,
    kind,
    floor,
    part,
    red,
    pv,
    stat,
    tails,
    pol_local,
    pol_send,
    pol_recv,
    own_local,
    scen_send,
    scen_recv,
    red_send,
    red_recv,
    pv_send,
    pv_recv,
    stat_send,
    stat_recv,
    tail_send,
    tail_recv,
    final,
    term_ref,
    cohort_ref,
    type_ref,
    floor_ref,
    strike_ref,
    small_local,
):
    z = lax.axis_index("blk")
    x = lax.axis_index("scen")
    core = lax.axis_index("month")
    other = 1 - core
    h = n // 2
    side = z // h
    low = h * jnp.where(core == 0, side, 1 - side)
    half, pols = cash_ref.shape
    months, lanes = disc_ref.shape
    types = strike_hbm.shape[0]
    depth = lhs.shape[2]
    first = -(-months // 32) * 16
    pieces = ((0, first), (first, months - first))
    chunks = [(a, k) for k in range(2) for a in range(2)]
    scen_total = n * nx * lanes
    peers = n * nx
    me = z * nx + x

    barrier = pltpu.get_barrier_semaphore()

    def greet(**where):
        pl.semaphore_signal(barrier, inc=1, device_id=where, device_id_type=MESH)

    greet(month=other)

    @pl.when(core == 0)
    def _():
        @pl.when(z > 0)
        def _():
            greet(blk=z - 1)

        @pl.when(z < n - 1)
        def _():
            greet(blk=z + 1)

    @pl.when(core == 1)
    def _():
        def peer(i, carry):
            to = lax.rem(me + i, peers)
            greet(blk=to // nx, scen=lax.rem(to, nx))
            return carry

        lax.fori_loop(1, peers, peer, 0)

        def line_peer(i, carry):
            greet(blk=lax.rem(z + i, n), month=jnp.int32(0))
            return carry

        lax.fori_loop(1, n, line_peer, 0)

    small = [
        pltpu.make_async_copy(src, dst, small_local.at[k])
        for k, (src, dst) in enumerate(
            (
                (term_hbm, term_ref),
                (cohort_hbm, cohort_ref),
                (type_hbm, type_ref),
                (floor_hbm, floor_ref),
                (strike_hbm, strike_ref),
            )
        )
    ]
    for copy in small:
        copy.start()
    own_pol = [
        pltpu.make_async_copy(ref, pol.at[core, a], pol_local.at[a])
        for a, ref in enumerate((cash_ref, fund_ref))
    ]
    for copy in own_pol:
        copy.start()
    mine = (z >= low) & (z < low + h)

    def own_scen(a):
        ref = (disc_ref, index_ref)[a]
        return pltpu.make_async_copy(ref, scen.at[z - low, a], own_local.at[a])

    @pl.when(mine)
    def _():
        for a in range(2):
            own_scen(a).start()

    around = jnp.where(z > 0, 1, 0) + jnp.where(z < n - 1, 1, 0)
    pl.semaphore_wait(barrier, jnp.where(core == 1, peers, n + around))

    def piece(ref, k):
        return ref.at[pl.ds(pieces[k][0], pieces[k][1])]

    def hop(src, j, a, k, right):
        return remote(
            piece(src, k),
            piece(scen.at[j, a], k),
            scen_send.at[j, a, k, right],
            scen_recv.at[j, a, k],
            blk=z + (1 if right else -1),
            month=jnp.where((z + (1 if right else -1)) // h == side, core, 1),
        )

    for a, k in chunks:
        ref = (disc_ref, index_ref)[a]

        @pl.when(mine & (z < n - 1))
        def _():
            hop(ref, z - low, a, k, 1).start()

        @pl.when(mine & (z > 0))
        def _():
            hop(ref, z - low, a, k, 0).start()

    give_pol = [
        remote(ref, pol.at[core, a], pol_send.at[a], pol_recv.at[a], month=other)
        for a, ref in enumerate((cash_ref, fund_ref))
    ]
    for copy in give_pol:
        copy.start()

    for copy in small:
        copy.wait()
    term = term_ref[...].reshape(1, pols)
    month = lax.broadcasted_iota(jnp.int32, (depth, pols), 0)
    in_force = month < term
    cohort_row = cohort_ref[...].reshape(1, pols)
    hot[...] = jnp.where(
        lax.broadcasted_iota(jnp.int32, (COHORTS, pols), 0) == cohort_row, 1.0, 0.0
    ).astype(BF16)
    kind[...] = jnp.broadcast_to(type_ref[...].reshape(1, pols).astype(F32), (lanes, pols)).T
    floor[...] = jnp.broadcast_to(floor_ref[...].astype(F32).reshape(1, pols), (lanes, pols)).T
    for a in range(2):
        own_pol[a].wait()
        remote(
            pol.at[other, a], pol.at[other, a], pol_send.at[a], pol_recv.at[a], month=other
        ).wait_recv()
        held = jnp.concatenate(
            [
                pol[0, a].astype(F32),
                pol[1, a].astype(F32),
                jnp.zeros((depth - months, pols), F32),
            ],
            axis=0,
        )
        lhs[a] = jnp.where(in_force, held, 0.0).T.astype(BF16)

    def cohort_terms(j):
        pad = jnp.zeros((depth - months, lanes), BF16)
        disc = jnp.concatenate([scen[j, 0], pad], axis=0)
        net = jnp.dot(lhs[0], disc, preferred_element_type=F32)
        index = scen[j, 1].astype(F32)
        pays = jnp.concatenate(
            [
                jnp.concatenate(
                    [jnp.maximum(strike_ref[t] - index, 0.0).astype(BF16), pad], axis=0
                )
                for t in range(types)
            ],
            axis=1,
        )
        every = jnp.dot(lhs[1], pays, preferred_element_type=F32)
        which = kind[...]
        guarantee = every[:, :lanes]
        for t in range(1, types):
            guarantee = jnp.where(which == t, every[:, t * lanes : (t + 1) * lanes], guarantee)
        value = jnp.maximum(net + guarantee, floor[...])
        high = value.astype(BF16)
        rest = value - high.astype(F32)
        middle = rest.astype(BF16)
        least = (rest - middle.astype(F32)).astype(BF16)
        sums = jnp.dot(
            hot[...], jnp.concatenate([high, middle, least], axis=1), preferred_element_type=F32
        )
        return sums[:, :lanes] + sums[:, lanes : 2 * lanes] + sums[:, 2 * lanes :]

    def give_red(j):
        return remote(
            part.at[j], red.at[z], red_send.at[j], red_recv.at[z], blk=low + j, month=jnp.int32(1)
        )

    def step(t, carry):
        d = (t + 1) // 2
        b = jnp.where(lax.rem(t, 2) == 1, z - d, z + d)
        j = b - low

        @pl.when((j >= 0) & (j < h))
        def _():
            @pl.when(b == z)
            def _():
                for a in range(2):
                    own_scen(a).wait()

            for a, k in chunks:
                @pl.when(b < z)
                def _():
                    hop(scen.at[j, a], j, a, k, 1).wait_recv()

                @pl.when(b > z)
                def _():
                    hop(scen.at[j, a], j, a, k, 0).wait_recv()

                @pl.when((b < z) & (z < n - 1))
                def _():
                    hop(scen.at[j, a], j, a, k, 1).start()

                @pl.when((b > z) & (z > 0))
                def _():
                    hop(scen.at[j, a], j, a, k, 0).start()

            sums = cohort_terms(j)
            part[j] = sums

            give_red(j).start()

        return carry

    lax.fori_loop(0, 2 * n - 1, step, 0)

    give_pv = remote(pv, pv, pv_send.at[0], pv_recv.at[0], month=other)
    give_final = remote(final, final, pv_send.at[1], pv_recv.at[1], month=other)

    def each(first, last, action):
        def go(i, carry):
            action(i)
            return carry

        lax.fori_loop(first, last, go, 0)

    def share(ref, send_sem, recv_sem, i, slot):
        to = lax.rem(me + i, peers)
        where = slot(to)
        return remote(
            ref.at[where],
            ref.at[where],
            send_sem.at[i],
            recv_sem.at[where],
            blk=to // nx,
            scen=lax.rem(to, nx),
        )

    def give(ref, send_sem, recv_sem, i):
        return share(ref, send_sem, recv_sem, i, lambda to: me)

    def take(ref, send_sem, recv_sem, i):
        return share(ref, send_sem, recv_sem, i, lambda to: to)

    @pl.when(core == 1)
    def _():
        def take_red(i):
            remote(red.at[i], red.at[i], red_send.at[0], red_recv.at[i], month=other).wait_recv()

        each(0, n, take_red)
        own = red[0]
        for i in range(1, n):
            own = own + red[i]
        own = own * scaling
        turned = jnp.concatenate([own, jnp.zeros((lanes - COHORTS, lanes), F32)], axis=0).T
        stat[me] = jnp.concatenate(
            [
                jnp.sum(turned, axis=0, keepdims=True),
                jnp.sum(turned * turned, axis=0, keepdims=True),
            ],
            axis=0,
        )
        each(1, peers, lambda i: give(stat, stat_send, stat_recv, i).start())
        pv[...] = own
        give_pv.start()
        pv_ref[...] = own
        each(1, peers, lambda i: take(stat, stat_send, stat_recv, i).wait_recv())
        stats = jnp.sum(stat[...], axis=0)
        centre = stats[0:1] / scen_total
        spread = stats[1:2] / scen_total - centre * centre
        temper = 0.5 * jnp.sqrt(spread + 1e-05)
        weights = jax.nn.sigmoid((turned - centre) / temper)
        tails[me] = jnp.concatenate(
            [
                jnp.sum(weights * turned, axis=0, keepdims=True),
                jnp.sum(weights, axis=0, keepdims=True),
            ],
            axis=0,
        )
        each(1, peers, lambda i: give(tails, tail_send, tail_recv, i).start())
        each(1, peers, lambda i: give(stat, stat_send, stat_recv, i).wait_send())
        give_pv.wait_send()
        each(1, peers, lambda i: take(tails, tail_send, tail_recv, i).wait_recv())
        ends = jnp.sum(tails[...], axis=0)
        final[...] = ends[0:1] / ends[1:2]
        give_final.start()

    for copy in give_pol:
        copy.wait_send()

    def finish(j, carry):
        b = low + j
        for a, k in chunks:
            @pl.when((b <= z) & (z < n - 1))
            def _():
                hop(scen.at[j, a], j, a, k, 1).wait_send()

            @pl.when((b >= z) & (z > 0))
            def _():
                hop(scen.at[j, a], j, a, k, 0).wait_send()

        give_red(j).wait_send()

        return carry

    lax.fori_loop(0, h, finish, 0)

    @pl.when(core == 1)
    def _():
        each(1, peers, lambda i: give(tails, tail_send, tail_recv, i).wait_send())
        give_final.wait_send()

    @pl.when(core == 0)
    def _():
        give_pv.wait_recv()
        pv_ref[...] = pv[...]
        give_final.wait_recv()

    tail_ref[...] = final[:, :COHORTS]


def per_device(
    cash_flow, fund_units, term_months, cohort, guar_type, surrender, discount, fund_index, strike
):
    n, nx = lax.axis_size("blk"), lax.axis_size("scen")
    half, pols = cash_flow.shape
    months, lanes = discount.shape
    h = n // 2
    peers = n * nx
    depth = -(-months // 256) * 256
    scaling = 1.0 / math.sqrt(pols * n / COHORTS)
    vmem = pl.BlockSpec(memory_space=pltpu.VMEM)
    hbm = pl.BlockSpec(memory_space=pltpu.HBM)
    dma = pltpu.SemaphoreType.DMA
    cohort_pv, tail = pl.pallas_call(
        functools.partial(kernel, n, nx, scaling),
        out_shape=(
            jax.ShapeDtypeStruct((COHORTS, lanes), F32),
            jax.ShapeDtypeStruct((1, COHORTS), F32),
        ),
        in_specs=[hbm] * 9,
        out_specs=(vmem, vmem),
        scratch_shapes=[
            pltpu.VMEM((2, 2, half, pols), BF16),
            pltpu.VMEM((h, 2, months, lanes), BF16),
            pltpu.VMEM((2, pols, depth), BF16),
            pltpu.VMEM((COHORTS, pols), BF16),
            pltpu.VMEM((pols, lanes), F32),
            pltpu.VMEM((pols, lanes), F32),
            pltpu.VMEM((h, COHORTS, lanes), F32),
            pltpu.VMEM((n, COHORTS, lanes), F32),
            pltpu.VMEM((COHORTS, lanes), F32),
            pltpu.VMEM((peers, 2, lanes), F32),
            pltpu.VMEM((peers, 2, lanes), F32),
            dma((2,)),
            dma((2,)),
            dma((2,)),
            dma((2,)),
            dma((h, 2, 2, 2)),
            dma((h, 2, 2)),
            dma((h,)),
            dma((n,)),
            dma((2,)),
            dma((2,)),
            dma((peers,)),
            dma((peers,)),
            dma((peers,)),
            dma((peers,)),
            pltpu.VMEM((1, lanes), F32),
            pltpu.VMEM((pols,), jnp.int32),
            pltpu.VMEM((pols,), jnp.int32),
            pltpu.VMEM((pols,), jnp.int32),
            pltpu.VMEM((pols,), BF16),
            pltpu.SMEM((strike.shape[0],), F32),
            dma((5,)),
        ],
        compiler_params=pltpu.CompilerParams(
            collective_id=0, has_side_effects=True, vmem_limit_bytes=56 * 1024 * 1024
        ),
        cost_estimate=pl.CostEstimate(
            flops=10 * pols * h * lanes * months, bytes_accessed=1 << 20, transcendentals=0
        ),
    )(
        cash_flow,
        fund_units,
        term_months,
        cohort,
        guar_type,
        surrender,
        discount,
        fund_index,
        strike,
    )
    return cohort_pv, tail.reshape(COHORTS)


def solution(mesh):
    return jax.shard_map(
        per_device,
        mesh=mesh,
        in_specs=(
            P("month", ("groups", "blk")),
            P("month", ("groups", "blk")),
            P(("groups", "blk")),
            P(("groups", "blk")),
            P(("groups", "blk")),
            P(("groups", "blk")),
            P(None, ("groups", "blk", "scen")),
            P(None, ("groups", "blk", "scen")),
            P(),
        ),
        out_specs=(P("groups", ("blk", "scen")), P("groups")),
        check_vma=False,
    )
```

```python
import functools
import math

import jax
import jax.numpy as jnp
from jax import lax
from jax.experimental import pallas as pl
from jax.experimental.pallas import tpu as pltpu
from jax.sharding import PartitionSpec as P

COHORTS = 64
MESH = pl.DeviceIdType.MESH
BF16 = jnp.bfloat16
F32 = jnp.float32


def remote(src, dst, send_sem, recv_sem, **where):
    return pltpu.make_async_remote_copy(
        src_ref=src,
        dst_ref=dst,
        send_sem=send_sem,
        recv_sem=recv_sem,
        device_id=where,
        device_id_type=MESH,
    )


def kernel(
    n,
    nx,
    scaling,
    cash_ref,
    fund_ref,
    term_hbm,
    cohort_hbm,
    type_hbm,
    floor_hbm,
    disc_ref,
    index_ref,
    strike_hbm,
    pv_ref,
    tail_ref,
    pol,
    scen,
    lhs,
    hot,
    kind,
    floor,
    part,
    red,
    pv,
    stat,
    tails,
    pol_local,
    pol_send,
    pol_recv,
    own_local,
    scen_send,
    scen_recv,
    red_send,
    red_recv,
    pv_send,
    pv_recv,
    stat_send,
    stat_recv,
    tail_send,
    tail_recv,
    final,
    term_ref,
    cohort_ref,
    type_ref,
    floor_ref,
    strike_ref,
    small_local,
    out_local,
):
    z = lax.axis_index("blk")
    x = lax.axis_index("scen")
    core = lax.axis_index("month")
    other = 1 - core
    h = n // 2
    side = z // h
    low = h * jnp.where(core == 0, side, 1 - side)
    half, pols = cash_ref.shape
    months, lanes = disc_ref.shape
    types = strike_hbm.shape[0]
    depth = lhs.shape[2]
    first = -(-months // 32) * 16
    pieces = ((0, first), (first, months - first))
    chunks = [(a, k) for k in range(2) for a in range(2)]
    scen_total = n * nx * lanes
    peers = n * nx
    me = z * nx + x

    barrier = pltpu.get_barrier_semaphore()

    def greet(**where):
        pl.semaphore_signal(barrier, inc=1, device_id=where, device_id_type=MESH)

    greet(month=other)

    @pl.when(core == 0)
    def _():
        @pl.when(z > 0)
        def _():
            greet(blk=z - 1)

        @pl.when(z < n - 1)
        def _():
            greet(blk=z + 1)

    @pl.when(core == 1)
    def _():
        def peer(i, carry):
            to = lax.rem(me + i, peers)
            greet(blk=to // nx, scen=lax.rem(to, nx))
            return carry

        lax.fori_loop(1, peers, peer, 0)

        def line_peer(i, carry):
            greet(blk=lax.rem(z + i, n), month=jnp.int32(0))
            return carry

        lax.fori_loop(1, n, line_peer, 0)

    small = [
        pltpu.make_async_copy(src, dst, small_local.at[k])
        for k, (src, dst) in enumerate(
            (
                (term_hbm, term_ref),
                (cohort_hbm, cohort_ref),
                (type_hbm, type_ref),
                (floor_hbm, floor_ref),
                (strike_hbm, strike_ref),
            )
        )
    ]
    for copy in small:
        copy.start()
    own_pol = [
        pltpu.make_async_copy(ref, pol.at[core, a], pol_local.at[a])
        for a, ref in enumerate((cash_ref, fund_ref))
    ]
    for copy in own_pol:
        copy.start()
    mine = (z >= low) & (z < low + h)

    def own_scen(a):
        ref = (disc_ref, index_ref)[a]
        return pltpu.make_async_copy(ref, scen.at[z - low, a], own_local.at[a])

    @pl.when(mine)
    def _():
        for a in range(2):
            own_scen(a).start()

    around = jnp.where(z > 0, 1, 0) + jnp.where(z < n - 1, 1, 0)
    pl.semaphore_wait(barrier, jnp.where(core == 1, peers, n + around))

    def piece(ref, k):
        return ref.at[pl.ds(pieces[k][0], pieces[k][1])]

    def hop(src, j, a, k, right):
        return remote(
            piece(src, k),
            piece(scen.at[j, a], k),
            scen_send.at[j, a, k, right],
            scen_recv.at[j, a, k],
            blk=z + (1 if right else -1),
            month=jnp.where((z + (1 if right else -1)) // h == side, core, 1),
        )

    for a, k in chunks:
        ref = (disc_ref, index_ref)[a]

        @pl.when(mine & (z < n - 1))
        def _():
            hop(ref, z - low, a, k, 1).start()

        @pl.when(mine & (z > 0))
        def _():
            hop(ref, z - low, a, k, 0).start()

    give_pol = [
        remote(ref, pol.at[core, a], pol_send.at[a], pol_recv.at[a], month=other)
        for a, ref in enumerate((cash_ref, fund_ref))
    ]
    for copy in give_pol:
        copy.start()

    for copy in small:
        copy.wait()
    term = term_ref[...].reshape(1, pols)
    month = lax.broadcasted_iota(jnp.int32, (depth, pols), 0)
    in_force = month < term
    cohort_row = cohort_ref[...].reshape(1, pols)
    hot[...] = jnp.where(
        lax.broadcasted_iota(jnp.int32, (COHORTS, pols), 0) == cohort_row, 1.0, 0.0
    ).astype(BF16)
    kind[...] = jnp.broadcast_to(type_ref[...].reshape(1, pols).astype(F32), (lanes, pols)).T
    floor[...] = jnp.broadcast_to(floor_ref[...].astype(F32).reshape(1, pols), (lanes, pols)).T
    for a in range(2):
        own_pol[a].wait()
        remote(
            pol.at[other, a], pol.at[other, a], pol_send.at[a], pol_recv.at[a], month=other
        ).wait_recv()
        held = jnp.concatenate(
            [
                pol[0, a].astype(F32),
                pol[1, a].astype(F32),
                jnp.zeros((depth - months, pols), F32),
            ],
            axis=0,
        )
        lhs[a] = jnp.where(in_force, held, 0.0).T.astype(BF16)

    def cohort_terms(j):
        pad = jnp.zeros((depth - months, lanes), BF16)
        disc = jnp.concatenate([scen[j, 0], pad], axis=0)
        net = jnp.dot(lhs[0], disc, preferred_element_type=F32)
        index = scen[j, 1].astype(F32)
        pays = jnp.concatenate(
            [
                jnp.concatenate(
                    [jnp.maximum(strike_ref[t] - index, 0.0).astype(BF16), pad], axis=0
                )
                for t in range(types)
            ],
            axis=1,
        )
        every = jnp.dot(lhs[1], pays, preferred_element_type=F32)
        which = kind[...]
        guarantee = every[:, :lanes]
        for t in range(1, types):
            guarantee = jnp.where(which == t, every[:, t * lanes : (t + 1) * lanes], guarantee)
        value = jnp.maximum(net + guarantee, floor[...])
        high = value.astype(BF16)
        rest = value - high.astype(F32)
        middle = rest.astype(BF16)
        least = (rest - middle.astype(F32)).astype(BF16)
        sums = jnp.dot(
            hot[...], jnp.concatenate([high, middle, least], axis=1), preferred_element_type=F32
        )
        return sums[:, :lanes] + sums[:, lanes : 2 * lanes] + sums[:, 2 * lanes :]

    def give_red(j):
        return remote(
            part.at[j], red.at[z], red_send.at[j], red_recv.at[z], blk=low + j, month=jnp.int32(1)
        )

    def step(t, carry):
        d = (t + 1) // 2
        b = jnp.where(lax.rem(t, 2) == 1, z - d, z + d)
        j = b - low

        @pl.when((j >= 0) & (j < h))
        def _():
            @pl.when(b == z)
            def _():
                for a in range(2):
                    own_scen(a).wait()

            for a, k in chunks:
                @pl.when(b < z)
                def _():
                    hop(scen.at[j, a], j, a, k, 1).wait_recv()

                @pl.when(b > z)
                def _():
                    hop(scen.at[j, a], j, a, k, 0).wait_recv()

                @pl.when((b < z) & (z < n - 1))
                def _():
                    hop(scen.at[j, a], j, a, k, 1).start()

                @pl.when((b > z) & (z > 0))
                def _():
                    hop(scen.at[j, a], j, a, k, 0).start()

            sums = cohort_terms(j)
            part[j] = sums

            give_red(j).start()

        return carry

    lax.fori_loop(0, 2 * n - 1, step, 0)

    out_pv = pltpu.make_async_copy(pv, pv_ref, out_local.at[0])
    give_pv = remote(pv, pv, pv_send.at[0], pv_recv.at[0], month=other)
    give_final = remote(final, final, pv_send.at[1], pv_recv.at[1], month=other)

    def each(first, last, action):
        def go(i, carry):
            action(i)
            return carry

        lax.fori_loop(first, last, go, 0)

    def share(ref, send_sem, recv_sem, i, slot):
        to = lax.rem(me + i, peers)
        where = slot(to)
        return remote(
            ref.at[where],
            ref.at[where],
            send_sem.at[i],
            recv_sem.at[where],
            blk=to // nx,
            scen=lax.rem(to, nx),
        )

    def give(ref, send_sem, recv_sem, i):
        return share(ref, send_sem, recv_sem, i, lambda to: me)

    def take(ref, send_sem, recv_sem, i):
        return share(ref, send_sem, recv_sem, i, lambda to: to)

    @pl.when(core == 1)
    def _():
        def take_red(i):
            remote(red.at[i], red.at[i], red_send.at[0], red_recv.at[i], month=other).wait_recv()

        each(0, n, take_red)
        own = red[0]
        for i in range(1, n):
            own = own + red[i]
        own = own * scaling
        turned = jnp.concatenate([own, jnp.zeros((lanes - COHORTS, lanes), F32)], axis=0).T
        stat[me] = jnp.concatenate(
            [
                jnp.sum(turned, axis=0, keepdims=True),
                jnp.sum(turned * turned, axis=0, keepdims=True),
            ],
            axis=0,
        )
        each(1, peers, lambda i: give(stat, stat_send, stat_recv, i).start())
        pv[...] = own
        give_pv.start()
        out_pv.start()
        each(1, peers, lambda i: take(stat, stat_send, stat_recv, i).wait_recv())
        stats = jnp.sum(stat[...], axis=0)
        centre = stats[0:1] / scen_total
        spread = stats[1:2] / scen_total - centre * centre
        temper = 0.5 * jnp.sqrt(spread + 1e-05)
        weights = jax.nn.sigmoid((turned - centre) / temper)
        tails[me] = jnp.concatenate(
            [
                jnp.sum(weights * turned, axis=0, keepdims=True),
                jnp.sum(weights, axis=0, keepdims=True),
            ],
            axis=0,
        )
        each(1, peers, lambda i: give(tails, tail_send, tail_recv, i).start())
        each(1, peers, lambda i: give(stat, stat_send, stat_recv, i).wait_send())
        give_pv.wait_send()
        each(1, peers, lambda i: take(tails, tail_send, tail_recv, i).wait_recv())
        ends = jnp.sum(tails[...], axis=0)
        final[...] = ends[0:1] / ends[1:2]
        give_final.start()

    @pl.when(core == 0)
    def _():
        give_pv.wait_recv()
        out_pv.start()

    for copy in give_pol:
        copy.wait_send()

    def finish(j, carry):
        b = low + j
        for a, k in chunks:
            @pl.when((b <= z) & (z < n - 1))
            def _():
                hop(scen.at[j, a], j, a, k, 1).wait_send()

            @pl.when((b >= z) & (z > 0))
            def _():
                hop(scen.at[j, a], j, a, k, 0).wait_send()

        give_red(j).wait_send()

        return carry

    lax.fori_loop(0, h, finish, 0)

    @pl.when(core == 1)
    def _():
        each(1, peers, lambda i: give(tails, tail_send, tail_recv, i).wait_send())
        give_final.wait_send()

    @pl.when(core == 0)
    def _():
        give_final.wait_recv()

    tail_ref[...] = final[:, :COHORTS]
    out_pv.wait()


def per_device(
    cash_flow, fund_units, term_months, cohort, guar_type, surrender, discount, fund_index, strike
):
    n, nx = lax.axis_size("blk"), lax.axis_size("scen")
    half, pols = cash_flow.shape
    months, lanes = discount.shape
    h = n // 2
    peers = n * nx
    depth = -(-months // 256) * 256
    scaling = 1.0 / math.sqrt(pols * n / COHORTS)
    vmem = pl.BlockSpec(memory_space=pltpu.VMEM)
    hbm = pl.BlockSpec(memory_space=pltpu.HBM)
    dma = pltpu.SemaphoreType.DMA
    cohort_pv, tail = pl.pallas_call(
        functools.partial(kernel, n, nx, scaling),
        out_shape=(
            jax.ShapeDtypeStruct((COHORTS, lanes), F32),
            jax.ShapeDtypeStruct((1, COHORTS), F32),
        ),
        in_specs=[hbm] * 9,
        out_specs=(hbm, vmem),
        scratch_shapes=[
            pltpu.VMEM((2, 2, half, pols), BF16),
            pltpu.VMEM((h, 2, months, lanes), BF16),
            pltpu.VMEM((2, pols, depth), BF16),
            pltpu.VMEM((COHORTS, pols), BF16),
            pltpu.VMEM((pols, lanes), F32),
            pltpu.VMEM((pols, lanes), F32),
            pltpu.VMEM((h, COHORTS, lanes), F32),
            pltpu.VMEM((n, COHORTS, lanes), F32),
            pltpu.VMEM((COHORTS, lanes), F32),
            pltpu.VMEM((peers, 2, lanes), F32),
            pltpu.VMEM((peers, 2, lanes), F32),
            dma((2,)),
            dma((2,)),
            dma((2,)),
            dma((2,)),
            dma((h, 2, 2, 2)),
            dma((h, 2, 2)),
            dma((h,)),
            dma((n,)),
            dma((2,)),
            dma((2,)),
            dma((peers,)),
            dma((peers,)),
            dma((peers,)),
            dma((peers,)),
            pltpu.VMEM((1, lanes), F32),
            pltpu.VMEM((pols,), jnp.int32),
            pltpu.VMEM((pols,), jnp.int32),
            pltpu.VMEM((pols,), jnp.int32),
            pltpu.VMEM((pols,), BF16),
            pltpu.SMEM((strike.shape[0],), F32),
            dma((5,)),
            dma((1,)),
        ],
        compiler_params=pltpu.CompilerParams(
            collective_id=0, has_side_effects=True, vmem_limit_bytes=56 * 1024 * 1024
        ),
        cost_estimate=pl.CostEstimate(
            flops=10 * pols * h * lanes * months, bytes_accessed=1 << 20, transcendentals=0
        ),
    )(
        cash_flow,
        fund_units,
        term_months,
        cohort,
        guar_type,
        surrender,
        discount,
        fund_index,
        strike,
    )
    return cohort_pv, tail.reshape(COHORTS)


def solution(mesh):
    return jax.shard_map(
        per_device,
        mesh=mesh,
        in_specs=(
            P("month", ("groups", "blk")),
            P("month", ("groups", "blk")),
            P(("groups", "blk")),
            P(("groups", "blk")),
            P(("groups", "blk")),
            P(("groups", "blk")),
            P(None, ("groups", "blk", "scen")),
            P(None, ("groups", "blk", "scen")),
            P(),
        ),
        out_specs=(P("groups", ("blk", "scen")), P("groups")),
        check_vma=False,
    )
```
